256 devices in a mesh: ctx: 16 (over x_hi, y, core), exp: 16 (over z, x_lo).
Axes of the slice: x: 4 (x_hi: 2, x_lo: 2; x = x_hi * 2 + x_lo), y: 4, z: 8, core: 2. Of those that a mesh axis runs over, the one named last changes fastest.
Arguments:
- queries: bfloat16 [2048, 12288], P('ctx', 'exp'), may hold values from -100 to 100
- kv_latent: bfloat16 [2048, 576], P('ctx'), may hold values from -8 to 8
- kv_up: bfloat16 [512, 16384], P(None, 'exp'), may hold values from -0.25 to 0.25
- out_proj: bfloat16 [8192, 7168], P('exp', 'ctx'), may hold values from -0.0625 to 0.0625
- residual: bfloat16 [2048, 7168], P(('ctx', 'exp')), may hold values from -6 to 6
- norm_gain: float32 [7168], replicated, may hold values from 0.1 to 1.9
- routes: int32 [2048, 4], P(('ctx', 'exp')), may hold values from 0 to 31, all different within a row; in each aligned block of 8 rows (0 to 7, 8 to 15, ...) at most 2 rows name the same one
- gate_scores: float32 [2048, 4], P(('ctx', 'exp')), may hold values from 0.05 to 1
- expert_gate_up: bfloat16 [16, 2, 7168, 2048], P('exp', None, None, 'ctx'), may hold values from -0.0625 to 0.0625
- expert_down: bfloat16 [16, 2048, 7168], P('exp', 'ctx'), may hold values from -0.1875 to 0.1875
- shared_gate_up: bfloat16 [2, 7168, 2048], P(None, None, 'ctx'), may hold values from -0.0625 to 0.0625
- shared_down: bfloat16 [2048, 7168], P('ctx'), may hold values from -0.125 to 0.125
Outputs:
- layer_out: bfloat16 [2048, 7168], P(('ctx', 'exp'))
The draws below stay inside these ranges and needn't reach their ends.
Inputs may be any that keep to these rules, and one draw needn't show every extreme that they name: `routes`: each row names 4 different experts; in each aligned block of 8 rows (the rows of one device) no expert is named by more than 2 rows, a bound that some block reaches.
All inputs are finite; a program needn't handle non-finite values.
Results may differ from the reference program's by a relative error of at most 0.027.
Values may be sent and summed in bfloat16 or wider, within the bound.
No kernel may reach another device: no remote copies, remote signals or barrier semaphores. Data moves between devices by JAX's collectives and lax.ppermute only.
A program may use at most 128 MiB of HBM per device.

```python
import math
import jax
import jax.numpy as jnp
import numpy as np
from jax import lax

D = 7168
HEADS_DEV = 4
NOPE = 128
ROPE = 64
VHD = 128
KVL = 512
FF_R = 1024
FF_S = 2048
TOPK = 4
HEADS = 64
EXPERTS = 32
SEQ = 2048
TOK_DEV = 8
CAP = 2
EXPERT_SLICE = 128
SHARED_SLICE = 128
N_CTX = 16
N_EXP = 16


def draw_kv_latent(key, part):
    key = jax.random.fold_in(key, 11)
    latent = jax.random.normal(jax.random.fold_in(key, 2), (SEQ, KVL + ROPE))
    return jnp.clip(latent, -8.0, 8.0).astype(jnp.bfloat16)


def draw_queries(key, part):
    key = jax.random.fold_in(key, 13)
    query_draw = jax.random.normal(jax.random.fold_in(key, 2), (SEQ, HEADS, NOPE + ROPE))
    query_draw = jnp.clip(query_draw, -100.0, 100.0)
    return query_draw.reshape(SEQ, HEADS * (NOPE + ROPE)).astype(jnp.bfloat16)


def level_of(stream_key, shape, shards, smallest, largest):
    def one(axis_at, parts):
        steps = jax.random.uniform(jax.random.fold_in(jax.random.fold_in(stream_key, 6), axis_at), (parts,), jnp.float32, smallest / len(shards), largest / len(shards))
        return jnp.repeat(jnp.exp(steps), shape[axis_at] // parts).reshape((-1,) + (1,) * (len(shape) - axis_at - 1))

    level = one(*shards[0])
    for cut in shards[1:]:
        level = level * one(*cut)
    return level


def shared_out(stream_key, own, number, rows, count, top, bound, slope):
    sequence = jax.random.permutation(stream_key, count)
    packed, usual = load_shares(count, rows * top, bound, slope, True), load_shares(count, rows * top, bound, slope, False)
    places = jnp.arange(count)

    def named(tallies, rotation):
        used = int((tallies > 0).sum())
        fixed = max(1, used // 4)
        shifted = fixed + (places - fixed + rotation * (used - fixed)) % max(1, count - fixed)
        return jnp.zeros((count,), jnp.int32).at[sequence[jnp.where(places < fixed, places, shifted)]].set(jnp.asarray(tallies, jnp.int32))

    tallies = jnp.where(number % 4 == 0, named(packed, number // 4), named(usual, number - number // 4 - 1))
    mixed = jax.random.permutation(jax.random.fold_in(own, 3), count)
    giver, sink = mixed[0:count // 2 * 2:2], mixed[1:count // 2 * 2:2]
    slack = jnp.minimum(tallies[giver] - 1, bound - tallies[sink]) // 2
    slack = jnp.where((giver == sequence[0]) | (sink == sequence[0]) | (tallies[sink] == 0), 0, jnp.maximum(slack, 0))
    shifted = jax.random.randint(jax.random.fold_in(own, 4), (count // 2,), 0, 1 << 20) % (slack + 1)
    tallies = tallies.at[giver].add(-shifted).at[sink].add(shifted)
    labels = jnp.searchsorted(jnp.cumsum(tallies), jnp.arange(rows * top), side="right").astype(jnp.int32)
    listing = labels.reshape(top, rows).T
    listing = listing[jax.random.permutation(jax.random.fold_in(own, 1), rows)]
    rotation = jax.random.randint(jax.random.fold_in(own, 2), (rows, 1), 0, top)
    return jnp.take_along_axis(listing, (jnp.arange(top)[None, :] + rotation) % top, axis=1)


def load_shares(number_of, total, bound, lean, full):
    weights = [(1 << 20) // math.isqrt(grade ** lean) + 1 for grade in range(1, number_of + 1)]
    largest = bound if full else min(bound, max(-(-total // number_of), total * weights[0] // sum(weights)))
    least = 1 if total - largest >= number_of - 1 else 0
    given, rest = [largest] + [least] * (number_of - 1), total - largest - least * (number_of - 1)
    while rest > 0:
        free = [i for i in range(1, number_of) if given[i] < largest] or [i for i in range(1, number_of) if given[i] < bound]
        mass, left = sum([weights[i] for i in free]), rest
        for i in free:
            extra = min(bound - given[i], max(1, left * weights[i] // mass), rest)
            given[i] = given[i] + extra
            rest = rest - extra
    return np.array(given)


def gaussian(own_key, dims, scale, limit, shards=(), held_as=jnp.bfloat16):
    values = jax.random.normal(own_key, dims, jnp.float32) * scale
    if len(shards) > 0:
        values = level_of(own_key, dims, shards, -0.22, 0.18) * values
    return jnp.clip(values, min=-limit, max=limit).astype(held_as)


def setup_inputs(seed: int = 0) -> dict:
    splits = jax.random.split(jax.random.key(seed), 13)
    queries = draw_queries(jax.random.fold_in(splits[12], 71), 0)
    kv_latent = draw_kv_latent(jax.random.fold_in(splits[12], 71), 0)
    kv_up = gaussian(splits[2], (KVL, HEADS * (NOPE + VHD)), KVL ** -0.5, 0.25, ((1, 16),))
    out_proj = gaussian(splits[3], (HEADS * VHD, D), (HEADS * VHD) ** -0.5, 0.0625, ((0, 16), (1, 16)))
    residual = gaussian(splits[4], (SEQ, D), 1.0, 6.0, ((0, 256),))
    norm_gain = jnp.clip(1.0 + 0.18 * jax.random.normal(splits[5], (D,), jnp.float32), 0.1, 1.9)
    routes_keys = jax.random.split(jax.random.fold_in(splits[6], 1), SEQ // TOK_DEV)
    routes_turns = jax.random.permutation(jax.random.fold_in(splits[6], 3), SEQ // TOK_DEV)
    routes = jax.vmap(lambda own, number: shared_out(jax.random.fold_in(splits[6], 2), own, number, TOK_DEV, EXPERTS, TOPK, CAP, 2))(routes_keys, routes_turns).reshape((SEQ, TOPK))
    gate_scores = jnp.clip(jnp.exp(math.log(1.0) - 2.9957323 * jax.random.uniform(splits[7], (SEQ, TOPK), jnp.float32) ** level_of(splits[7], (SEQ, TOPK), ((0, 256),), -0.2, 0.2)), 0.05, 1.0)
    expert_gate_up = gaussian(splits[8], (EXPERTS // 2, 2, D, 2 * FF_R), D ** -0.5, 0.0625, ((0, 16), (3, 16)))
    expert_down = gaussian(splits[9], (EXPERTS // 2, 2 * FF_R, D), FF_R ** -0.5, 0.1875, ((0, 16), (1, 16)))
    shared_gate_up = gaussian(splits[10], (2, D, FF_S), D ** -0.5, 0.0625, ((2, 16),))
    shared_down = gaussian(splits[11], (FF_S, D), FF_S ** -0.5, 0.125, ((0, 16),))
    return dict(queries=queries, kv_latent=kv_latent, kv_up=kv_up, out_proj=out_proj, residual=residual, norm_gain=norm_gain, routes=routes, gate_scores=gate_scores, expert_gate_up=expert_gate_up, expert_down=expert_down, shared_gate_up=shared_gate_up, shared_down=shared_down)


def rounded(values):
    return lax.optimization_barrier(values.astype(jnp.bfloat16)).astype(jnp.float32)

def swiglu(row_block, gate_proj, up_proj):
    gate_part = jnp.dot(row_block, gate_proj, preferred_element_type=jnp.float32)
    up_part = jnp.dot(row_block, up_proj, preferred_element_type=jnp.float32)
    return (jax.nn.silu(gate_part) * up_part).astype(jnp.bfloat16)

def reference(queries, kv_latent, kv_up, out_proj, residual, norm_gain, routes, gate_scores, expert_gate_up, expert_down, shared_gate_up, shared_down):
    keys_values = jnp.dot(kv_latent[:, :KVL], kv_up, preferred_element_type=jnp.float32).astype(jnp.bfloat16)
    rope_keys = kv_latent[:, KVL:]
    positions = jnp.arange(SEQ, dtype=jnp.int32)
    allowed = positions[None, :] <= positions[:, None]

    def one_head(head_index):
        query_cols = lax.dynamic_slice_in_dim(queries, head_index * (NOPE + ROPE), NOPE + ROPE, 1)
        head_block = lax.dynamic_slice_in_dim(keys_values, head_index * (NOPE + VHD), NOPE + VHD, 1)
        key_full = jnp.concatenate([head_block[:, :NOPE], rope_keys], axis=1)
        scores = jnp.dot(query_cols, key_full.T, preferred_element_type=jnp.float32) / math.sqrt(NOPE + ROPE)
        row_max = lax.optimization_barrier(jnp.max(jnp.where(allowed, scores, -jnp.inf), axis=1, keepdims=True))
        weights = jnp.exp(jnp.where(allowed, scores - row_max, -jnp.inf))
        probabilities = weights.astype(jnp.bfloat16)
        weighted_sum = jnp.dot(probabilities, head_block[:, NOPE:], preferred_element_type=jnp.float32)
        return (weighted_sum / lax.optimization_barrier(jnp.sum(weights, axis=1, keepdims=True))).astype(jnp.bfloat16)
    attended = lax.map(one_head, jnp.arange(HEADS, dtype=jnp.int32))
    attended = jnp.transpose(attended, (1, 0, 2)).reshape(SEQ, HEADS * VHD)
    group_width = HEADS_DEV * VHD

    def add_group(group_index, summed):
        offset = (group_index * group_width).astype(jnp.int32)
        group_cols = lax.dynamic_slice_in_dim(attended, offset, group_width, 1)
        group_rows = lax.dynamic_slice_in_dim(out_proj, offset, group_width, 0)
        return summed + rounded(jnp.dot(group_cols, group_rows, preferred_element_type=jnp.float32))
    head_total = lax.fori_loop(0, N_EXP, add_group, jnp.zeros((SEQ, D), jnp.float32))
    hidden = (residual.astype(jnp.float32) + head_total).astype(jnp.bfloat16)
    hidden_f = hidden.astype(jnp.float32)
    normed = (hidden_f * lax.rsqrt(lax.optimization_barrier(jnp.mean(hidden_f * hidden_f, axis=1, keepdims=True)) + 1e-06) * norm_gain).astype(jnp.bfloat16)
    shared_act = swiglu(normed, shared_gate_up[0], shared_gate_up[1])

    def add_shared(slice_index, summed):
        offset = (slice_index * SHARED_SLICE).astype(jnp.int32)
        act_block = lax.dynamic_slice_in_dim(shared_act, offset, SHARED_SLICE, 1)
        down_block = lax.dynamic_slice_in_dim(shared_down, offset, SHARED_SLICE, 0)
        return summed + rounded(jnp.dot(act_block, down_block, preferred_element_type=jnp.float32))
    shared_total = lax.fori_loop(0, N_CTX, add_shared, jnp.zeros((SEQ, D), jnp.float32))
    route_weight = 2.5 * gate_scores / lax.optimization_barrier(jnp.sum(gate_scores, axis=1, keepdims=True))
    blocks = SEQ // TOK_DEV
    flat_routes = routes.reshape(blocks, TOK_DEV * TOPK)
    expert_ids = jnp.arange(EXPERTS, dtype=jnp.int32)
    onehot = (flat_routes[:, :, None] == expert_ids[None, None, :]).astype(jnp.int32)
    rank_within = lax.optimization_barrier(jnp.sum((jnp.cumsum(onehot, axis=1) - 1) * onehot, axis=2))
    block_ids = jnp.arange(blocks, dtype=jnp.int32)[:, None]
    slot_index = (flat_routes * (blocks * CAP) + block_ids * CAP + rank_within).reshape(-1).astype(jnp.int32)
    token_rows = jnp.repeat(normed, TOPK, axis=0)
    buffer = jnp.zeros((EXPERTS * blocks * CAP, D), jnp.bfloat16).at[slot_index].set(token_rows)
    buffer = buffer.reshape(EXPERTS, blocks * CAP, D)

    def one_expert(expert):
        pair_index = expert // 2
        offset = (expert % 2 * FF_R).astype(jnp.int32)
        gate_proj = lax.dynamic_slice_in_dim(expert_gate_up[pair_index, 0], offset, FF_R, 1)
        up_proj = lax.dynamic_slice_in_dim(expert_gate_up[pair_index, 1], offset, FF_R, 1)
        down_rows = lax.dynamic_slice_in_dim(expert_down[pair_index], offset, FF_R, 0)
        routed_act = swiglu(buffer[expert], gate_proj, up_proj)

        def add_block(slice_index, summed):
            inner = (slice_index * EXPERT_SLICE).astype(jnp.int32)
            act_block = lax.dynamic_slice_in_dim(routed_act, inner, EXPERT_SLICE, 1)
            down_block = lax.dynamic_slice_in_dim(down_rows, inner, EXPERT_SLICE, 0)
            return summed + rounded(jnp.dot(act_block, down_block, preferred_element_type=jnp.float32))
        summed = lax.fori_loop(0, FF_R // EXPERT_SLICE, add_block, jnp.zeros((blocks * CAP, D), jnp.float32))
        return summed.astype(jnp.bfloat16)
    expert_out = lax.map(one_expert, expert_ids)
    picked = expert_out.reshape(-1, D)[slot_index].reshape(SEQ, TOPK, D).astype(jnp.float32)
    routed_total = lax.optimization_barrier(jnp.sum(route_weight[:, :, None] * picked, axis=1))
    return (hidden_f + shared_total + routed_total).astype(jnp.bfloat16)
```

```python
import math

import jax
import jax.numpy as jnp
from jax import lax
from jax.sharding import PartitionSpec as P

D = 7168
NOPE = 128
ROPE = 64
VHD = 128
KVL = 512
TOPK = 4


def swiglu(row_block, gate_proj, up_proj):
    gate_part = jnp.dot(row_block, gate_proj, preferred_element_type=jnp.float32)
    up_part = jnp.dot(row_block, up_proj, preferred_element_type=jnp.float32)
    return (jax.nn.silu(gate_part) * up_part).astype(jnp.bfloat16)


def on_device(
    queries,
    kv_latent,
    kv_up,
    out_proj,
    residual,
    norm_gain,
    routes,
    gate_scores,
    expert_gate_up,
    expert_down,
    shared_gate_up,
    shared_down,
):
    ctx_count = lax.axis_size("ctx")
    exp_count = lax.axis_size("exp")
    tok_block = queries.shape[0]
    heads_local = queries.shape[1] // (NOPE + ROPE)
    seq_total = tok_block * ctx_count
    query_heads = queries.reshape(tok_block, heads_local, NOPE + ROPE)
    shard_piece = lax.all_gather(kv_latent, "ctx", axis=0, tiled=True)
    piece_rows = shard_piece.shape[0]
    expanded = jnp.dot(shard_piece[:, :KVL], kv_up, preferred_element_type=jnp.float32).astype(
        jnp.bfloat16
    )
    expanded = expanded.reshape(piece_rows, heads_local, NOPE + VHD)
    rope_part = jnp.broadcast_to(shard_piece[:, None, KVL:], (piece_rows, heads_local, ROPE))
    key_full = jnp.concatenate([expanded[:, :, :NOPE], rope_part], axis=2)
    block_scores = jnp.einsum(
        "qhc,khc->hqk", query_heads, key_full, preferred_element_type=jnp.float32
    ) / math.sqrt(NOPE + ROPE)
    value_all = expanded[:, :, NOPE:]
    query_pos = lax.axis_index("ctx") * tok_block + jnp.arange(tok_block, dtype=jnp.int32)
    key_pos = jnp.arange(seq_total, dtype=jnp.int32)
    allowed = (key_pos[None, :] <= query_pos[:, None])[None, :, :]
    row_max = jnp.max(jnp.where(allowed, block_scores, -jnp.inf), axis=2, keepdims=True)
    weights = jnp.exp(jnp.where(allowed, block_scores - row_max, -jnp.inf))
    probabilities = weights.astype(jnp.bfloat16)
    weighted_sum = jnp.einsum(
        "hqk,khv->qhv", probabilities, value_all, preferred_element_type=jnp.float32
    )
    normalizer = jnp.sum(weights, axis=2).T[:, :, None]
    attended = (
        (weighted_sum / normalizer).astype(jnp.bfloat16).reshape(tok_block, heads_local * VHD)
    )
    projected = jnp.dot(
        attended,
        lax.all_gather(out_proj, "ctx", axis=1, tiled=True),
        preferred_element_type=jnp.float32,
    ).astype(jnp.bfloat16)
    head_total = lax.psum_scatter(
        lax.optimization_barrier(projected).astype(jnp.float32).astype(jnp.bfloat16),
        "exp",
        scatter_dimension=0,
        tiled=True,
    ).astype(jnp.float32)
    hidden = (residual.astype(jnp.float32) + head_total).astype(jnp.bfloat16)
    hidden_f = hidden.astype(jnp.float32)
    normed = (
        hidden_f
        * lax.rsqrt(jnp.mean(hidden_f * hidden_f, axis=1, keepdims=True) + 1e-06)
        * norm_gain
    ).astype(jnp.bfloat16)
    tok_local = residual.shape[0]
    experts = 2 * exp_count
    capacity = min(tok_local, 2 * tok_local * TOPK // experts)
    flat_routes = routes.reshape(-1)
    order = jnp.arange(flat_routes.shape[0], dtype=jnp.int32)
    earlier = (flat_routes[:, None] == flat_routes[None, :]) & (order[None, :] < order[:, None])
    rank_within = jnp.sum(earlier.astype(jnp.int32), axis=1)
    slot_index = (flat_routes * capacity + rank_within).reshape(tok_local, TOPK)
    slot_ids = jnp.arange(experts * capacity, dtype=jnp.int32)
    matches = slot_index[None, :, :] == slot_ids[:, None, None]
    placement = jnp.any(matches, axis=2).astype(jnp.bfloat16)
    send_rows = jnp.dot(placement, normed, preferred_element_type=jnp.float32).astype(jnp.bfloat16)
    send_rows = send_rows.reshape(exp_count, 2, capacity, D)
    received = lax.all_to_all(send_rows, "exp", split_axis=0, concat_axis=0, tiled=True)
    by_half = jnp.transpose(received, (1, 0, 2, 3)).reshape(2, exp_count * capacity, D)
    routed_send = jnp.repeat(by_half, ctx_count // 2, axis=0)
    shared_send = jnp.broadcast_to(normed[None], (ctx_count, tok_local, D))
    routed_in, shared_in = (
        lax.all_to_all(routed_send, "ctx", split_axis=0, concat_axis=0, tiled=True),
        lax.all_to_all(shared_send, "ctx", split_axis=0, concat_axis=0, tiled=True),
    )
    routed_act = swiglu(routed_in.reshape(-1, D), expert_gate_up[0, 0], expert_gate_up[0, 1])
    routed_part = jnp.dot(routed_act, expert_down[0], preferred_element_type=jnp.float32).astype(
        jnp.bfloat16
    )
    routed_part = routed_part.reshape(ctx_count, exp_count * capacity, D)
    shared_act = swiglu(shared_in.reshape(-1, D), shared_gate_up[0], shared_gate_up[1])
    shared_part = jnp.dot(shared_act, shared_down, preferred_element_type=jnp.float32).astype(
        jnp.bfloat16
    )
    shared_part = shared_part.reshape(ctx_count, tok_local, D)
    back_routed, back_shared = (
        lax.all_to_all(routed_part, "ctx", split_axis=0, concat_axis=0, tiled=True),
        lax.all_to_all(shared_part, "ctx", split_axis=0, concat_axis=0, tiled=True),
    )
    summed_parts = (
        back_routed.astype(jnp.float32)
        .reshape(2, ctx_count // 2, exp_count, capacity, D)
        .sum(axis=1)
    )
    expert_out = jnp.transpose(summed_parts, (1, 0, 2, 3)).astype(jnp.bfloat16)
    returned = lax.all_to_all(expert_out, "exp", split_axis=0, concat_axis=0, tiled=True).reshape(
        experts * capacity, D
    )
    route_weight = 2.5 * gate_scores / jnp.sum(gate_scores, axis=1, keepdims=True)
    weight_table = jnp.sum(jnp.where(matches, route_weight[None, :, :], 0.0), axis=2).T
    routed_total = jnp.dot(
        weight_table, returned.astype(jnp.float32), precision=lax.Precision.HIGHEST
    )
    shared_total = back_shared.astype(jnp.float32).sum(axis=0)
    return (hidden_f + shared_total + routed_total).astype(jnp.bfloat16)


def solution(mesh):
    return jax.shard_map(
        on_device,
        mesh=mesh,
        in_specs=(
            P("ctx", "exp"),
            P("ctx", None),
            P(None, "exp"),
            P("exp", "ctx"),
            P(("ctx", "exp"), None),
            P(),
            P(("ctx", "exp"), None),
            P(("ctx", "exp"), None),
            P("exp", None, None, "ctx"),
            P("exp", "ctx", None),
            P(None, None, "ctx"),
            P("ctx", None),
        ),
        out_specs=P(("ctx", "exp"), None),
        check_vma=False,
    )
```

```python
import math

import jax
import jax.numpy as jnp
from jax import lax
from jax.sharding import Mesh
from jax.sharding import PartitionSpec as P

D = 7168
NOPE = 128
ROPE = 64
VHD = 128
KVL = 512
TOPK = 4
BF = jnp.bfloat16
F32 = jnp.float32
AXES = ("xh", "y", "core", "z", "xl")
CTX = ("xh", "y", "core")
EXP = ("z", "xl")


def swap(x, axis):
    return lax.ppermute(x, axis, [(0, 1), (1, 0)])


def to_next(x, axis):
    n = lax.axis_size(axis)
    return lax.ppermute(x, axis, [(i, (i + 1) % n) for i in range(n)])


def to_prev(x, axis):
    n = lax.axis_size(axis)
    return lax.ppermute(x, axis, [(i, (i - 1) % n) for i in range(n)])


def ring4(x):
    half = x.shape[0] // 2
    from_prev = to_next(x, "y")
    from_next = to_prev(x, "y")
    far = jnp.concatenate([to_next(from_prev[:half], "y"), to_prev(from_next[half:], "y")], axis=0)
    return [x, from_next, far, from_prev]


def add(a, b):
    return (a.astype(F32) + b.astype(F32)).astype(BF)


def reduce4(own, nxt, far, prv):
    half = own.shape[0] // 2
    nxt = jnp.concatenate([add(nxt[:half], to_next(far[:half], "y")), nxt[half:]], axis=0)
    prv = jnp.concatenate([prv[:half], add(prv[half:], to_prev(far[half:], "y"))], axis=0)
    return own.astype(F32) + to_next(nxt, "y").astype(F32) + to_prev(prv, "y").astype(F32)


def reduce_z(parts):
    ahead = to_next(parts[4][:, :8], "z")
    back = to_prev(parts[4][:, 8:], "z")
    up = jnp.concatenate([add(parts[3][:, :8], ahead), parts[3][:, 8:]], axis=1)
    down = jnp.concatenate([parts[5][:, :8], add(parts[5][:, 8:], back)], axis=1)
    for a, b in ((2, 6), (1, 7)):
        up = add(parts[a], to_next(up, "z"))
        down = add(parts[b], to_prev(down, "z"))
    return parts[0].astype(F32) + to_next(up, "z").astype(F32) + to_prev(down, "z").astype(F32)


def swiglu(rows, gate_proj, up_proj):
    gate_part = jnp.dot(rows, gate_proj, preferred_element_type=F32)
    up_part = jnp.dot(rows, up_proj, preferred_element_type=F32)
    return (jax.nn.silu(gate_part) * up_part).astype(BF)


def attention(queries, kv_latent, kv_up):
    tok = queries.shape[0]
    heads = queries.shape[1] // (NOPE + ROPE)
    xh, y, core = (lax.axis_index(a) for a in CTX)
    pair = jnp.concatenate([kv_latent, swap(kv_latent, "xh")], axis=0)
    chip = ring4(pair)
    latent = jnp.concatenate(chip + [swap(p, "core") for p in chip], axis=0)
    starts = []
    for c in (core, 1 - core):
        for dy in range(4):
            for x in (xh, 1 - xh):
                starts.append((x * 8 + lax.rem(y + dy, 4) * 2 + c) * tok)
    starts = jnp.stack(starts)
    key_pos = (starts[:, None] + jnp.arange(tok, dtype=jnp.int32)[None, :]).reshape(-1)
    query_heads = queries.reshape(tok, heads, NOPE + ROPE)
    seq = latent.shape[0]
    expanded = jnp.dot(latent[:, :KVL], kv_up, preferred_element_type=F32).astype(BF)
    expanded = expanded.reshape(seq, heads, NOPE + VHD)
    rope_part = jnp.broadcast_to(latent[:, None, KVL:], (seq, heads, ROPE))
    key_full = jnp.concatenate([expanded[:, :, :NOPE], rope_part], axis=2)
    scores = jnp.einsum(
        "qhc,khc->hqk", query_heads, key_full, preferred_element_type=F32
    ) / math.sqrt(NOPE + ROPE)
    query_pos = (xh * 8 + y * 2 + core) * tok + jnp.arange(tok, dtype=jnp.int32)
    allowed = (key_pos[None, :] <= query_pos[:, None])[None, :, :]
    row_max = jnp.max(jnp.where(allowed, scores, -jnp.inf), axis=2, keepdims=True)
    weights = jnp.exp(jnp.where(allowed, scores - row_max, -jnp.inf))
    weighted = jnp.einsum(
        "hqk,khv->qhv", weights.astype(BF), expanded[:, :, NOPE:], preferred_element_type=F32
    )
    total = jnp.sum(weights, axis=2).T[:, :, None]
    return (weighted / total).astype(BF).reshape(tok, heads * VHD)


def project(attended, out_proj):
    xh, y, core, z, xl = (lax.axis_index(a) for a in AXES)
    half = out_proj.shape[0] // 2
    kept = lax.dynamic_slice_in_dim(out_proj, core * half, half, 0)
    other = swap(lax.dynamic_slice_in_dim(out_proj, (1 - core) * half, half, 0), "core")
    first = core == 0
    mine = jnp.concatenate([jnp.where(first, kept, other), jnp.where(first, other, kept)], axis=1)
    width = mine.shape[1]
    pair = jnp.stack([mine, swap(mine, "xh")])
    chip = ring4(pair)
    tok = attended.shape[0]
    rolled = lax.dynamic_slice_in_dim(
        jnp.concatenate([attended, attended], axis=0), z * (tok // 8), tok, 0
    )
    low, high = rolled[:, :half], rolled[:, half:]
    att_own, att_other = jnp.where(first, low, high), jnp.where(first, high, low)
    sums = []
    for group in ((0, 1), (2, 3)):
        blocks = []
        for i in group:
            theirs = swap(chip[i], "core")
            for j in range(2):
                blocks.append(
                    (
                        jnp.dot(att_own, chip[i][j], preferred_element_type=F32)
                        + jnp.dot(att_other, theirs[j], preferred_element_type=F32)
                    ).astype(BF)
                )
        stacked = jnp.stack(blocks).reshape(len(blocks), 8, tok // 8, width)
        rows = reduce_z([stacked[:, d] for d in range(8)]).astype(BF)
        low_rows, high_rows = rows[:, : tok // 16], rows[:, tok // 16 :]
        mine_rows = jnp.where(xl == 0, low_rows, high_rows)
        sent = jnp.where(xl == 0, high_rows, low_rows)
        sums.append(mine_rows.astype(F32) + swap(sent, "xl").astype(F32))
    total = jnp.concatenate(sums, axis=0).reshape(4, 2, tok // 16, width)
    total = jnp.where(xh == 0, total, total[:, ::-1])
    total = lax.dynamic_slice_in_dim(jnp.concatenate([total, total], axis=0), lax.rem(4 - y, 4), 4, 0)
    return jnp.transpose(total, (2, 1, 0, 3)).reshape(tok // 16, D)


def on_device(
    queries,
    kv_latent,
    kv_up,
    out_proj,
    residual,
    norm_gain,
    routes,
    gate_scores,
    expert_gate_up,
    expert_down,
    shared_gate_up,
    shared_down,
):
    attended = attention(queries, kv_latent, kv_up)
    head_total = project(attended, out_proj)
    hidden = (residual.astype(F32) + head_total).astype(BF)
    hidden_f = hidden.astype(F32)
    normed = (
        hidden_f
        * lax.rsqrt(jnp.mean(hidden_f * hidden_f, axis=1, keepdims=True) + 1e-06)
        * norm_gain
    ).astype(BF)
    tok_local = residual.shape[0]
    experts = 2 * lax.axis_size(EXP)
    capacity = min(tok_local, 2 * tok_local * TOPK // experts)
    flat_routes = routes.reshape(-1)
    order = jnp.arange(flat_routes.shape[0], dtype=jnp.int32)
    earlier = (flat_routes[:, None] == flat_routes[None, :]) & (order[None, :] < order[:, None])
    rank_within = jnp.sum(earlier.astype(jnp.int32), axis=1)
    slot_index = (flat_routes * capacity + rank_within).reshape(tok_local, TOPK)
    slots = experts * capacity
    slot_ids = jnp.arange(slots, dtype=jnp.int32)
    matches = slot_index[None, :, :] == slot_ids[:, None, None]
    placement = jnp.any(matches, axis=2).astype(BF)
    send_rows = jnp.dot(placement, normed, preferred_element_type=F32).astype(BF)
    plane = ("z", "xl", "xh")
    routed_own = lax.all_to_all(send_rows, plane, split_axis=0, concat_axis=0, tiled=True)
    rows = jnp.concatenate([routed_own, normed, swap(normed, "xh")], axis=0)
    ours = ring4(rows)
    parts = [None] * 4
    for group in ((0,), (1, 3), (2,)):
        blocks = [b for i in group for b in (ours[i], swap(ours[i], "core"))]
        routed_act = swiglu(
            jnp.concatenate([b[:slots] for b in blocks], axis=0),
            expert_gate_up[0, 0],
            expert_gate_up[0, 1],
        )
        routed_part = jnp.dot(routed_act, expert_down[0], preferred_element_type=F32).astype(BF)
        shared_act = swiglu(
            jnp.concatenate([b[slots:] for b in blocks], axis=0),
            shared_gate_up[0],
            shared_gate_up[1],
        )
        shared_part = jnp.dot(shared_act, shared_down, preferred_element_type=F32).astype(BF)
        routed_part = routed_part.reshape(len(group), 2, slots, D)
        shared_part = shared_part.reshape(len(group), 2, 2 * tok_local, D)
        for j, i in enumerate(group):
            keep = jnp.concatenate([routed_part[j, 0], shared_part[j, 0]], axis=0)
            give = jnp.concatenate([routed_part[j, 1], shared_part[j, 1]], axis=0)
            parts[i] = add(keep, swap(give, "core"))
    summed = reduce4(*parts)
    expert_out = summed[:slots].astype(BF)
    returned = lax.all_to_all(expert_out, plane, split_axis=0, concat_axis=0, tiled=True)
    peer_sum = swap(summed[slots + tok_local :].astype(BF), "xh").astype(F32)
    shared_total = summed[slots : slots + tok_local] + peer_sum
    route_weight = 2.5 * gate_scores / jnp.sum(gate_scores, axis=1, keepdims=True)
    weight_table = jnp.sum(jnp.where(matches, route_weight[None, :, :], 0.0), axis=2).T
    routed_total = jnp.dot(weight_table, returned.astype(F32), precision=lax.Precision.HIGHEST)
    return (hidden_f + shared_total + routed_total).astype(BF)


def solution(mesh):
    grid = Mesh(mesh.devices.reshape(2, 4, 2, 8, 2), AXES)
    return jax.shard_map(
        on_device,
        mesh=grid,
        in_specs=(
            P(CTX, EXP),
            P(CTX, None),
            P(None, EXP),
            P(EXP, CTX),
            P(CTX + EXP, None),
            P(),
            P(CTX + EXP, None),
            P(CTX + EXP, None),
            P(EXP, None, None, CTX),
            P(EXP, CTX, None),
            P(None, None, CTX),
            P(CTX, None),
        ),
        out_specs=P(CTX + EXP, None),
        check_vma=False,
    )
```

```python
import functools
import math

import jax
import jax.numpy as jnp
from jax import lax
from jax.experimental import pallas as pl
from jax.experimental.pallas import tpu as pltpu
from jax.sharding import Mesh
from jax.sharding import PartitionSpec as P

D = 7168
NOPE = 128
ROPE = 64
VHD = 128
KVL = 512
TOPK = 4
BF = jnp.bfloat16
F32 = jnp.float32
AXES = ("xh", "y", "core", "z", "xl")
CTX = ("xh", "y", "core")
EXP = ("z", "xl")
PLANE = ("z", "xl", "xh")
K_STEP = 1792
N_STEP = 1792


def swap(x, axis):
    return lax.ppermute(x, axis, [(0, 1), (1, 0)])


def shift(x, axis, by):
    n = lax.axis_size(axis)
    return lax.ppermute(x, axis, [(i, (i + by) % n) for i in range(n)])


def near_x(x):
    return lax.ppermute(x, ("xh", "xl"), [(0, 3), (3, 0), (1, 2), (2, 1)])


def all_to_all(x, axes):
    return lax.all_to_all(x, axes, split_axis=0, concat_axis=0, tiled=True)


def gather_y(x):
    return [x, shift(x, "y", -1), shift(x, "y", 2), shift(x, "y", 1)]


def add(a, b):
    return (a.astype(F32) + b.astype(F32)).astype(BF)


def expert_kernel(in_rows, out_rows, cuts, out_cuts, n_after, *refs):
    n_in, n_out = len(in_rows) * cuts, len(out_rows) * out_cuts
    x_refs = refs[:n_in]
    gu_ref, down_ref = refs[n_in : n_in + 2]
    outs_at = n_in + 2 + n_after
    out_refs = refs[outs_at : outs_at + n_out]
    x_v, gu_v, down_v, x_sem, gu_sem, down_sem = refs[outs_at + n_out :]
    width = D // cuts
    steps = D // K_STEP
    hidden = down_ref.shape[0]
    x_copies, gu_copies = [], []
    for c in range(cuts):
        offset = 0
        for b, rows in enumerate(in_rows):
            copy = pltpu.make_async_copy(
                x_refs[b * cuts + c], x_v.at[c, pl.ds(offset, rows), :], x_sem.at[b * cuts + c]
            )
            copy.start()
            x_copies.append(copy)
            offset += rows
        for s in range(c * steps // cuts, (c + 1) * steps // cuts):
            span = pl.ds(s * K_STEP, K_STEP)
            copy = pltpu.make_async_copy(gu_ref.at[:, span, :], gu_v.at[:, span, :], gu_sem.at[s])
            copy.start()
            gu_copies.append(copy)
    down_copy = pltpu.make_async_copy(down_ref, down_v, down_sem)
    down_copy.start()
    acc = None
    for s in range(steps):
        c = s * cuts // steps
        if s * cuts % steps == 0:
            for copy in x_copies[c * len(in_rows) : (c + 1) * len(in_rows)]:
                copy.wait()
        gu_copies[s].wait()
        lo = s * K_STEP - c * width
        both = jnp.concatenate(
            [gu_v[0, s * K_STEP : (s + 1) * K_STEP, :], gu_v[1, s * K_STEP : (s + 1) * K_STEP, :]],
            axis=1,
        )
        part = jnp.dot(x_v[c, :, lo : lo + K_STEP], both, preferred_element_type=F32)
        acc = part if acc is None else acc + part
    gate, up = acc[:, :hidden], acc[:, hidden:]
    act = (gate / (1.0 + jnp.exp(-gate)) * up).astype(BF)
    down_copy.wait()
    for s in range(D // N_STEP):
        c = s * N_STEP * out_cuts // D
        lo = s * N_STEP - c * (D // out_cuts)
        out = jnp.dot(
            act, down_v[:, s * N_STEP : (s + 1) * N_STEP], preferred_element_type=F32
        ).astype(BF)
        offset = 0
        for b, rows in enumerate(out_rows):
            out_refs[b * out_cuts + c][:, lo : lo + N_STEP] = out[offset : offset + rows]
            offset += rows


def expert_blocks(blocks, out_rows, out_cuts, gate_up, down, after=()):
    cuts = len(blocks[0])
    in_rows = tuple(b[0].shape[0] for b in blocks)
    rows = sum(in_rows)
    hidden = down.shape[0]
    steps = D // K_STEP
    flat = pl.pallas_call(
        functools.partial(expert_kernel, in_rows, out_rows, cuts, out_cuts, len(after)),
        out_shape=[
            jax.ShapeDtypeStruct((r, D // out_cuts), BF) for r in out_rows for _ in range(out_cuts)
        ],
        in_specs=[pl.BlockSpec(memory_space=pl.ANY)] * (len(in_rows) * cuts + 2 + len(after)),
        out_specs=[pl.BlockSpec(memory_space=pltpu.VMEM)] * (len(out_rows) * out_cuts),
        scratch_shapes=[
            pltpu.VMEM((cuts, rows, D // cuts), BF),
            pltpu.VMEM((2, D, hidden), BF),
            pltpu.VMEM((hidden, D), BF),
            pltpu.SemaphoreType.DMA((len(in_rows) * cuts,)),
            pltpu.SemaphoreType.DMA((steps,)),
            pltpu.SemaphoreType.DMA,
        ],
        compiler_params=pltpu.CompilerParams(vmem_limit_bytes=40 * 2**20),
        cost_estimate=pl.CostEstimate(
            flops=6 * rows * D * hidden,
            bytes_accessed=2 * (3 * D * hidden + 2 * rows * D),
            transcendentals=rows * hidden,
        ),
    )(*[part for b in blocks for part in b], gate_up, down, *after)
    return [flat[i * out_cuts : (i + 1) * out_cuts] for i in range(len(out_rows))]


def attention(queries, kv_latent, kv_up, sent):
    tok = queries.shape[0]
    heads = queries.shape[1] // (NOPE + ROPE)
    xh, y, core = (lax.axis_index(a) for a in CTX)
    pair = jnp.concatenate([kv_latent, near_x(kv_latent)], axis=0)
    chip = gather_y(pair)
    latent = jnp.concatenate(chip + [swap(p, "core") for p in chip], axis=0)
    latent, *sent = lax.optimization_barrier((latent, *sent))
    starts = []
    for c in (core, 1 - core):
        for dy in range(4):
            for x in (xh, 1 - xh):
                starts.append((x * 8 + lax.rem(y + dy, 4) * 2 + c) * tok)
    starts = jnp.stack(starts)
    key_pos = (starts[:, None] + jnp.arange(tok, dtype=jnp.int32)[None, :]).reshape(-1)
    query_heads = queries.reshape(tok, heads, NOPE + ROPE)
    seq = latent.shape[0]
    expanded = jnp.dot(latent[:, :KVL], kv_up, preferred_element_type=F32).astype(BF)
    expanded = expanded.reshape(seq, heads, NOPE + VHD)
    rope_part = jnp.broadcast_to(latent[:, None, KVL:], (seq, heads, ROPE))
    key_full = jnp.concatenate([expanded[:, :, :NOPE], rope_part], axis=2)
    scores = jnp.einsum(
        "qhc,khc->hqk", query_heads, key_full, preferred_element_type=F32
    ) / math.sqrt(NOPE + ROPE)
    query_pos = (xh * 8 + y * 2 + core) * tok + jnp.arange(tok, dtype=jnp.int32)
    allowed = (key_pos[None, :] <= query_pos[:, None])[None, :, :]
    row_max = jnp.max(jnp.where(allowed, scores, -jnp.inf), axis=2, keepdims=True)
    weights = jnp.exp(jnp.where(allowed, scores - row_max, -jnp.inf))
    weighted = jnp.einsum(
        "hqk,khv->qhv", weights.astype(BF), expanded[:, :, NOPE:], preferred_element_type=F32
    )
    total = jnp.sum(weights, axis=2).T[:, :, None]
    return (weighted / total).astype(BF).reshape(tok, heads * VHD), sent


def send_weights(out_proj):
    core = lax.axis_index("core")
    half = out_proj.shape[0] // 2
    first = core == 0
    kept = lax.dynamic_slice_in_dim(out_proj, core * half, half, 0)
    other = swap(lax.dynamic_slice_in_dim(out_proj, (1 - core) * half, half, 0), "core")
    mine = jnp.concatenate([jnp.where(first, kept, other), jnp.where(first, other, kept)], axis=1)
    a = lax.ppermute(mine, ("xh", "xl"), [(1, 0), (3, 1), (0, 2), (2, 3)])
    b = lax.ppermute(mine, ("xh", "xl"), [(2, 1), (1, 2)])
    return mine, a, b


def out_weights(mine, a, b):
    xh, core, xl = (lax.axis_index(i) for i in ("xh", "core", "xl"))
    first = core == 0
    x = 2 * xh + xl
    low = jnp.where(x == 0, mine, jnp.where(x == 1, b, a))
    high = jnp.where(x == 3, mine, jnp.where(x == 2, b, a))
    pair = jnp.concatenate([low, high], axis=0)
    theirs = swap(pair, "core")
    return jnp.concatenate([jnp.where(first, pair, theirs), jnp.where(first, theirs, pair)], axis=0)


def project(attended, weights):
    y, xl = lax.axis_index("y"), lax.axis_index("xl")
    n_y, n_z, n_xl = (lax.axis_size(a) for a in ("y", "z", "xl"))
    tok, depth = attended.shape
    half = depth // 2
    peer = swap(attended, "xl")
    left, right = jnp.where(xl == 0, attended, peer), jnp.where(xl == 0, peer, attended)
    both = jnp.concatenate(
        [left[:, :half], right[:, :half], left[:, half:], right[:, half:]], axis=1
    )
    rows = jnp.stack(gather_y(both)).reshape(n_y, n_z, tok // n_z, 2 * depth)
    rows = jnp.transpose(rows, (1, 0, 2, 3)).reshape(n_y * tok, 2 * depth)
    partial = jnp.dot(rows, weights, preferred_element_type=F32).astype(BF)
    width = partial.shape[1]
    partial = all_to_all(partial.reshape(n_z, n_y * tok // n_z, width), ("z",))
    summed = jnp.sum(partial.astype(F32), axis=0).astype(BF)
    local = summed.shape[0] // (n_y * n_xl)
    summed = summed.reshape(n_y, n_xl, local, width)
    ours = jnp.where(xl == 0, summed[:, 0], summed[:, 1])
    theirs = swap(jnp.where(xl == 0, summed[:, 1], summed[:, 0]), "xl")
    cols = jnp.stack([jnp.where(xl == 0, ours, theirs), jnp.where(xl == 0, theirs, ours)], axis=1)
    cols = cols.reshape(n_y, n_xl * local, width)
    mine = jnp.stack(
        [cols[0], shift(cols[3], "y", -1), shift(cols[2], "y", 2), shift(cols[1], "y", 1)]
    ).reshape(n_y, n_xl, local, width)
    mine = lax.dynamic_slice_in_dim(
        jnp.concatenate([mine, mine], axis=0), lax.rem(n_y - y, n_y), n_y, 0
    )
    return jnp.transpose(mine, (2, 1, 0, 3)).reshape(local, D)


def routed_ring(own, gate_up, down):
    left, right = own
    rows = left.shape[0]

    def other_core(block):
        return [swap(h, "core") for h in block]

    from_prev = [shift(left, "y", 1), shift(right, "y", 1)]
    from_next = [shift(left, "y", -1), shift(right, "y", -1)]
    far = [shift(from_prev[0], "y", 1), shift(from_next[1], "y", -1)]
    (keep,), (give,) = expert_blocks([own, other_core(own)], (rows, rows), 1, gate_up, down)
    from_next, from_prev, keep = lax.optimization_barrier((from_next, from_prev, keep))
    here = keep.astype(F32) + swap(give, "core").astype(F32)
    (keep_n,), (keep_p,), (give_np,) = expert_blocks(
        [from_next, from_prev, other_core(from_next), other_core(from_prev)],
        (rows, rows, 2 * rows),
        1,
        gate_up,
        down,
        after=(keep,),
    )
    far, keep_n = lax.optimization_barrier((far, keep_n))
    got = swap(give_np, "core")
    to_next, to_prev = add(keep_n, got[:rows]), add(keep_p, got[rows:])
    keep, give = expert_blocks(
        [far, other_core(far)], (rows, rows), 2, gate_up, down, after=(keep_n,)
    )
    to_far = [add(k, swap(g, "core")) for k, g in zip(keep, give, strict=True)]
    half = to_next.shape[1] // 2
    via_next, via_prev = shift(to_far[0], "y", 1), shift(to_far[1], "y", -1)
    to_next = jnp.concatenate([add(to_next[:, :half], via_next), to_next[:, half:]], axis=1)
    to_prev = jnp.concatenate([to_prev[:, :half], add(to_prev[:, half:], via_prev)], axis=1)
    total = here + shift(to_next, "y", 1).astype(F32) + shift(to_prev, "y", -1).astype(F32)
    return total.astype(BF)


def shared_parts(normed, gate_up, down):
    rows = jnp.concatenate([normed, near_x(normed)], axis=0)
    blocks = gather_y(rows)
    theirs = swap(jnp.concatenate(blocks, axis=0), "core")
    count = theirs.shape[0]
    (keep,), (give,) = expert_blocks(
        [[b] for b in blocks] + [[theirs]], (count, count), 1, gate_up, down
    )
    return keep, give


def shared_sum(parts, local):
    parts = parts.reshape(4, 2 * local, D)
    total = (
        parts[0].astype(F32)
        + shift(parts[1], "y", 1).astype(F32)
        + shift(parts[2], "y", 2).astype(F32)
        + shift(parts[3], "y", -1).astype(F32)
    )
    return total[:local] + near_x(total[local:].astype(BF)).astype(F32)


def on_device(
    queries,
    kv_latent,
    kv_up,
    out_proj,
    residual,
    norm_gain,
    routes,
    gate_scores,
    expert_gate_up,
    expert_down,
    shared_gate_up,
    shared_down,
):
    attended, sent = attention(queries, kv_latent, kv_up, send_weights(out_proj))
    head_total = project(attended, out_weights(*sent))
    hidden = (residual.astype(F32) + head_total.astype(F32)).astype(BF)
    hidden_f = hidden.astype(F32)
    normed = (
        hidden_f
        * lax.rsqrt(jnp.mean(hidden_f * hidden_f, axis=1, keepdims=True) + 1e-06)
        * norm_gain
    ).astype(BF)
    tok_local = residual.shape[0]
    experts = 2 * lax.axis_size(EXP)
    capacity = min(tok_local, 2 * tok_local * TOPK // experts)
    flat_routes = routes.reshape(-1)
    order = jnp.arange(flat_routes.shape[0], dtype=jnp.int32)
    earlier = (flat_routes[:, None] == flat_routes[None, :]) & (order[None, :] < order[:, None])
    rank_within = jnp.sum(earlier.astype(jnp.int32), axis=1)
    slot_index = (flat_routes * capacity + rank_within).reshape(tok_local, TOPK)
    slots = experts * capacity
    slot_ids = jnp.arange(slots, dtype=jnp.int32)
    matches = slot_index[None, :, :] == slot_ids[:, None, None]
    placement = jnp.any(matches, axis=2).astype(BF)
    send_rows = jnp.dot(placement, normed, preferred_element_type=F32).astype(BF)
    routed_own = all_to_all(send_rows, PLANE)
    keep, give = shared_parts(normed, shared_gate_up, shared_down)
    routed_own, keep, give = lax.optimization_barrier((routed_own, keep, give))
    parts = add(keep, swap(give, "core"))
    halves = [routed_own[:, : D // 2], routed_own[:, D // 2 :]]
    expert_out = routed_ring(halves, expert_gate_up[0], expert_down[0])
    expert_out, parts = lax.optimization_barrier((expert_out, parts))
    returned = all_to_all(expert_out, PLANE)
    shared_total = shared_sum(parts, tok_local)
    route_weight = 2.5 * gate_scores / jnp.sum(gate_scores, axis=1, keepdims=True)
    weight_table = jnp.sum(jnp.where(matches, route_weight[None, :, :], 0.0), axis=2).T
    routed_total = jnp.dot(weight_table, returned.astype(F32), precision=lax.Precision.HIGHEST)
    return (hidden_f + shared_total + routed_total).astype(BF)


def solution(mesh):
    grid = Mesh(mesh.devices.reshape(2, 4, 2, 8, 2), AXES)
    return jax.shard_map(
        on_device,
        mesh=grid,
        in_specs=(
            P(CTX, EXP),
            P(CTX, None),
            P(None, EXP),
            P(EXP, CTX),
            P(CTX + EXP, None),
            P(),
            P(CTX + EXP, None),
            P(CTX + EXP, None),
            P(EXP, None, None, CTX),
            P(EXP, CTX, None),
            P(None, None, CTX),
            P(CTX, None),
        ),
        out_specs=P(CTX + EXP, None),
        check_vma=False,
    )
```

```python
import functools
import math

import jax
import jax.numpy as jnp
from jax import lax
from jax.experimental import pallas as pl
from jax.experimental.pallas import tpu as pltpu
from jax.sharding import Mesh
from jax.sharding import PartitionSpec as P

D = 7168
NOPE = 128
ROPE = 64
VHD = 128
KVL = 512
TOPK = 4
BF = jnp.bfloat16
F32 = jnp.float32
AXES = ("xh", "y", "core", "z", "xl")
CTX = ("xh", "y", "core")
EXP = ("z", "xl")
PLANE = ("z", "xl", "xh")
STEP = 1792
CHUNKS = D // STEP


def swap(x, axis):
    return lax.ppermute(x, axis, [(0, 1), (1, 0)])


def shift(x, axis, by):
    n = lax.axis_size(axis)
    return lax.ppermute(x, axis, [(i, (i + by) % n) for i in range(n)])


def flip(x, axis, bits):
    return lax.ppermute(x, axis, [(i, i ^ bits) for i in range(lax.axis_size(axis))])


def near_x(x):
    return lax.ppermute(x, ("xh", "xl"), [(0, 3), (3, 0), (1, 2), (2, 1)])


def all_to_all(x, axes):
    return lax.all_to_all(x, axes, split_axis=0, concat_axis=0, tiled=True)


def gather_y(x):
    return [x, shift(x, "y", -1), shift(x, "y", 2), shift(x, "y", 1)]


def add(a, b):
    return (a.astype(F32) + b.astype(F32)).astype(BF)


def expert_kernel(in_rows, out_rows, cuts, out_cuts, n_after, *refs):
    n_in, n_out = len(in_rows) * cuts, len(out_rows) * out_cuts
    x_refs = refs[:n_in]
    gu_ref, down_ref = refs[n_in : n_in + 2]
    outs_at = n_in + 2 + n_after
    out_refs = refs[outs_at : outs_at + n_out]
    x_v, gu_v, down_v, x_sem, gu_sem, down_sem = refs[outs_at + n_out :]
    chunks, _, width = x_v.shape
    part_chunks = chunks // cuts
    steps = D // STEP
    hidden = down_ref.shape[0]
    x_copies, gu_copies = [], []
    for c in range(cuts):
        offset = 0
        for b, rows in enumerate(in_rows):
            copy = pltpu.make_async_copy(
                x_refs[b * cuts + c],
                x_v.at[pl.ds(c * part_chunks, part_chunks), pl.ds(offset, rows), :],
                x_sem.at[b * cuts + c],
            )
            copy.start()
            x_copies.append(copy)
            offset += rows
        for s in range(c * steps // cuts, (c + 1) * steps // cuts):
            span = pl.ds(s * STEP, STEP)
            copy = pltpu.make_async_copy(gu_ref.at[:, span, :], gu_v.at[:, span, :], gu_sem.at[s])
            copy.start()
            gu_copies.append(copy)
    down_copy = pltpu.make_async_copy(down_ref, down_v, down_sem)
    down_copy.start()
    acc = None
    for s in range(steps):
        if s * cuts % steps == 0:
            c = s * cuts // steps
            for copy in x_copies[c * len(in_rows) : (c + 1) * len(in_rows)]:
                copy.wait()
        gu_copies[s].wait()
        span = slice(s * STEP, (s + 1) * STEP)
        both = jnp.concatenate([gu_v[0, span, :], gu_v[1, span, :]], axis=1)
        chunk, lo = divmod(s * STEP, width)
        part = jnp.dot(x_v[chunk, :, lo : lo + STEP], both, preferred_element_type=F32)
        acc = part if acc is None else acc + part
    gate, up = acc[:, :hidden], acc[:, hidden:]
    act = (gate / (1.0 + jnp.exp(-gate)) * up).astype(BF)
    down_copy.wait()
    for s in range(steps):
        out = jnp.dot(
            act, down_v[:, s * STEP : (s + 1) * STEP], preferred_element_type=F32
        ).astype(BF)
        chunk, lo = divmod(s * STEP, width)
        part, chunk = divmod(chunk, chunks // out_cuts)
        offset = 0
        for b, rows in enumerate(out_rows):
            out_refs[b * out_cuts + part][chunk, :, lo : lo + STEP] = out[offset : offset + rows]
            offset += rows


def expert_blocks(blocks, out_rows, out_cuts, gate_up, down, after=()):
    cuts = len(blocks[0])
    in_rows = tuple(b[0].shape[1] for b in blocks)
    rows = sum(in_rows)
    hidden = down.shape[0]
    steps = D // STEP
    width = blocks[0][0].shape[2]
    chunks = D // width
    flat = pl.pallas_call(
        functools.partial(expert_kernel, in_rows, out_rows, cuts, out_cuts, len(after)),
        out_shape=[
            jax.ShapeDtypeStruct((chunks // out_cuts, r, width), BF)
            for r in out_rows
            for _ in range(out_cuts)
        ],
        in_specs=[pl.BlockSpec(memory_space=pl.ANY)] * (len(in_rows) * cuts)
        + [pl.BlockSpec(memory_space=pltpu.HBM)] * 2
        + [pl.BlockSpec(memory_space=pl.ANY)] * len(after),
        out_specs=[pl.BlockSpec(memory_space=pltpu.VMEM)] * (len(out_rows) * out_cuts),
        scratch_shapes=[
            pltpu.VMEM((chunks, rows, width), BF),
            pltpu.VMEM((2, D, hidden), BF),
            pltpu.VMEM((hidden, D), BF),
            pltpu.SemaphoreType.DMA((len(in_rows) * cuts,)),
            pltpu.SemaphoreType.DMA((steps,)),
            pltpu.SemaphoreType.DMA,
        ],
        compiler_params=pltpu.CompilerParams(vmem_limit_bytes=40 * 2**20),
        cost_estimate=pl.CostEstimate(
            flops=6 * rows * D * hidden,
            bytes_accessed=2 * (3 * D * hidden + 2 * rows * D),
            transcendentals=rows * hidden,
        ),
    )(*[part for b in blocks for part in b], gate_up, down, *after)
    return [flat[i * out_cuts : (i + 1) * out_cuts] for i in range(len(out_rows))]


def attention(queries, kv_latent, kv_up, sent):
    tok = queries.shape[0]
    heads = queries.shape[1] // (NOPE + ROPE)
    xh, y, core = (lax.axis_index(a) for a in CTX)
    pair = jnp.concatenate([kv_latent, near_x(kv_latent)], axis=0)
    chip = gather_y(pair)
    latent = jnp.concatenate(chip + [swap(p, "core") for p in chip], axis=0)
    latent, *sent = lax.optimization_barrier((latent, *sent))
    starts = []
    for c in (core, 1 - core):
        for dy in range(4):
            for x in (xh, 1 - xh):
                starts.append((x * 8 + lax.rem(y + dy, 4) * 2 + c) * tok)
    starts = jnp.stack(starts)
    key_pos = (starts[:, None] + jnp.arange(tok, dtype=jnp.int32)[None, :]).reshape(-1)
    query_heads = queries.reshape(tok, heads, NOPE + ROPE)
    seq = latent.shape[0]
    expanded = jnp.dot(latent[:, :KVL], kv_up, preferred_element_type=F32).astype(BF)
    expanded = expanded.reshape(seq, heads, NOPE + VHD)
    rope_part = jnp.broadcast_to(latent[:, None, KVL:], (seq, heads, ROPE))
    key_full = jnp.concatenate([expanded[:, :, :NOPE], rope_part], axis=2)
    scores = jnp.einsum(
        "qhc,khc->hqk", query_heads, key_full, preferred_element_type=F32
    ) / math.sqrt(NOPE + ROPE)
    query_pos = (xh * 8 + y * 2 + core) * tok + jnp.arange(tok, dtype=jnp.int32)
    allowed = (key_pos[None, :] <= query_pos[:, None])[None, :, :]
    row_max = jnp.max(jnp.where(allowed, scores, -jnp.inf), axis=2, keepdims=True)
    weights = jnp.exp(jnp.where(allowed, scores - row_max, -jnp.inf))
    weighted = jnp.einsum(
        "hqk,khv->qhv", weights.astype(BF), expanded[:, :, NOPE:], preferred_element_type=F32
    )
    total = jnp.sum(weights, axis=2).T[:, :, None]
    return (weighted / total).astype(BF).reshape(tok, heads * VHD), sent


def send_weights(out_proj):
    core = lax.axis_index("core")
    half = out_proj.shape[0] // 2
    first = core == 0
    kept = lax.dynamic_slice_in_dim(out_proj, core * half, half, 0)
    other = swap(lax.dynamic_slice_in_dim(out_proj, (1 - core) * half, half, 0), "core")
    mine = jnp.concatenate([jnp.where(first, kept, other), jnp.where(first, other, kept)], axis=1)
    a = lax.ppermute(mine, ("xh", "xl"), [(1, 0), (3, 1), (0, 2), (2, 3)])
    b = lax.ppermute(mine, ("xh", "xl"), [(2, 1), (1, 2)])
    return mine, a, b


def out_weights(mine, a, b):
    xh, core, xl = (lax.axis_index(i) for i in ("xh", "core", "xl"))
    first = core == 0
    x = 2 * xh + xl
    low = jnp.where(x == 0, mine, jnp.where(x == 1, b, a))
    high = jnp.where(x == 3, mine, jnp.where(x == 2, b, a))
    pair = jnp.concatenate([low, high], axis=0)
    theirs = swap(pair, "core")
    return jnp.concatenate([jnp.where(first, pair, theirs), jnp.where(first, theirs, pair)], axis=0)


def project(attended, weights):
    y, xl = lax.axis_index("y"), lax.axis_index("xl")
    n_y, n_z, n_xl = (lax.axis_size(a) for a in ("y", "z", "xl"))
    tok, depth = attended.shape
    half = depth // 2
    peer = swap(attended, "xl")
    left, right = jnp.where(xl == 0, attended, peer), jnp.where(xl == 0, peer, attended)
    both = jnp.concatenate(
        [left[:, :half], right[:, :half], left[:, half:], right[:, half:]], axis=1
    )
    rows = jnp.stack([both, *(flip(both, "y", j) for j in (1, 2, 3))]).reshape(n_y, n_z, tok // n_z, 2 * depth)
    rows = jnp.transpose(rows, (1, 0, 2, 3)).reshape(n_y * tok, 2 * depth)
    partial = jnp.dot(rows, weights, preferred_element_type=F32).astype(BF)
    width = partial.shape[1]
    partial = all_to_all(partial.reshape(n_z, n_y * tok // n_z, width), ("z",))
    summed = jnp.sum(partial.astype(F32), axis=0).astype(BF)
    local = summed.shape[0] // (n_y * n_xl)
    summed = summed.reshape(n_y, n_xl, local, width)
    ours = jnp.where(xl == 0, summed[:, 0], summed[:, 1])
    theirs = swap(jnp.where(xl == 0, summed[:, 1], summed[:, 0]), "xl")
    cols = jnp.stack([jnp.where(xl == 0, ours, theirs), jnp.where(xl == 0, theirs, ours)], axis=1)
    met = flip(jnp.stack([cols[1], cols[3]]), "y", 1)
    met_far = flip(jnp.stack([cols[2], met[1]]), "y", 2)
    mine = jnp.stack([cols[0], met[0], met_far[0], met_far[1]])
    mine = jnp.where(y % 2 == 0, mine, jnp.stack([mine[1], mine[0], mine[3], mine[2]]))
    mine = jnp.where(y < 2, mine, jnp.concatenate([mine[2:], mine[:2]], axis=0))
    return jnp.transpose(mine, (2, 1, 0, 3)).reshape(local, D)


def routed_ring(own, gate_up, down, early):
    left, right = own
    rows = left.shape[1]

    def other_core(block):
        return [swap(h, "core") for h in block]

    from_prev = [shift(left, "y", 1), shift(right, "y", 1)]
    from_next = [shift(left, "y", -1), shift(right, "y", -1)]
    far = [shift(from_prev[0], "y", 1), shift(from_next[1], "y", -1)]
    (keep,), (give,) = expert_blocks([own, other_core(own)], (rows, rows), 1, gate_up, down)
    from_next, from_prev, keep, early = lax.optimization_barrier((from_next, from_prev, keep, early))
    here = keep.astype(F32) + swap(give, "core").astype(F32)
    keep_n, keep_p, give_np = expert_blocks(
        [from_next, from_prev, other_core(from_next), other_core(from_prev)],
        (rows, rows, 2 * rows),
        2,
        gate_up,
        down,
        after=(keep,),
    )
    far, keep_n = lax.optimization_barrier((far, keep_n))
    got = other_core(give_np)
    to_next = [add(keep_n[c], got[c][:, :rows]) for c in range(2)]
    to_prev = [add(keep_p[c], got[c][:, rows:]) for c in range(2)]
    right_sum, left_sum = shift(to_next[1], "y", 1), shift(to_prev[0], "y", -1)
    keep, give = expert_blocks(
        [far, other_core(far)], (rows, rows), 2, gate_up, down, after=(keep_n[0],)
    )
    to_far = [add(k, g) for k, g in zip(keep, other_core(give), strict=True)]
    via_next, via_prev = shift(to_far[0], "y", 1), shift(to_far[1], "y", -1)
    next_left, prev_right = add(to_next[0], via_next), add(to_prev[1], via_prev)
    half = here.shape[0] // 2
    out_left = here[:half] + left_sum.astype(F32) + shift(next_left, "y", 1).astype(F32)
    out_right = here[half:] + right_sum.astype(F32) + shift(prev_right, "y", -1).astype(F32)
    return jnp.concatenate([out_left, out_right], axis=0).astype(BF), early


def shared_parts(normed, gate_up, down):
    rows = jnp.concatenate([normed, near_x(normed)], axis=0)
    blocks = gather_y(rows)
    theirs = swap(jnp.concatenate(blocks, axis=0), "core")
    count = theirs.shape[0]
    (keep,), (give,) = expert_blocks(
        [[b[None]] for b in [*blocks, theirs]], (count, count), 1, gate_up, down
    )
    return keep[0], give[0]


def shared_sum(parts, local):
    parts = parts.reshape(4, 2 * local, D)
    total = (
        parts[0].astype(F32)
        + shift(parts[1], "y", 1).astype(F32)
        + shift(parts[2], "y", 2).astype(F32)
        + shift(parts[3], "y", -1).astype(F32)
    )
    return total[:local] + near_x(total[local:].astype(BF)).astype(F32)


def on_device(
    queries,
    kv_latent,
    kv_up,
    out_proj,
    residual,
    norm_gain,
    routes,
    gate_scores,
    expert_gate_up,
    expert_down,
    shared_gate_up,
    shared_down,
):
    attended, sent = attention(queries, kv_latent, kv_up, send_weights(out_proj))
    head_total = project(attended, out_weights(*sent))
    hidden = (residual.astype(F32) + head_total.astype(F32)).astype(BF)
    hidden_f = hidden.astype(F32)
    normed = (
        hidden_f
        * lax.rsqrt(jnp.mean(hidden_f * hidden_f, axis=1, keepdims=True) + 1e-06)
        * norm_gain
    ).astype(BF)
    tok_local = residual.shape[0]
    experts = 2 * lax.axis_size(EXP)
    capacity = min(tok_local, 2 * tok_local * TOPK // experts)
    flat_routes = routes.reshape(-1)
    order = jnp.arange(flat_routes.shape[0], dtype=jnp.int32)
    earlier = (flat_routes[:, None] == flat_routes[None, :]) & (order[None, :] < order[:, None])
    rank_within = jnp.sum(earlier.astype(jnp.int32), axis=1)
    slot_index = (flat_routes * capacity + rank_within).reshape(tok_local, TOPK)
    slots = experts * capacity
    slot_ids = jnp.arange(slots, dtype=jnp.int32)
    matches = slot_index[None, :, :] == slot_ids[:, None, None]
    placement = jnp.any(matches, axis=2).astype(BF)
    same_chunk = jnp.eye(CHUNKS, dtype=BF)
    pick = placement.reshape(experts, 1, capacity, 1, tok_local) * same_chunk[None, :, None, :, None]
    chunked = jnp.transpose(normed.reshape(tok_local, CHUNKS, STEP), (1, 0, 2)).reshape(-1, STEP)
    send_rows = jnp.dot(
        pick.reshape(CHUNKS * slots, CHUNKS * tok_local), chunked, preferred_element_type=F32
    ).astype(BF)
    per_peer = CHUNKS * capacity
    arrived = all_to_all(send_rows.reshape(experts, per_peer, STEP), PLANE)
    arrived = arrived.reshape(CHUNKS * slots, STEP)
    at = jnp.arange(CHUNKS * slots, dtype=jnp.int32)
    peer_at = at % slots // capacity * per_peer + at // slots * capacity + at % capacity
    by_chunk = (peer_at[:, None] == at[None, :]).astype(BF)
    half = CHUNKS // 2 * slots
    halves = [
        jnp.dot(rows, arrived, preferred_element_type=F32).astype(BF).reshape(-1, slots, STEP)
        for rows in (by_chunk[:half], by_chunk[half:])
    ]
    early = shared_parts(normed, shared_gate_up, shared_down)
    expert_out, (keep, give) = routed_ring(halves, expert_gate_up[0], expert_down[0], early)
    parts = add(keep, swap(give, "core"))
    expert_out, parts = lax.optimization_barrier((expert_out, parts))
    by_peer = (at[:, None] == peer_at[None, :]).astype(BF)
    expert_out = jnp.dot(
        by_peer, expert_out.reshape(CHUNKS * slots, STEP), preferred_element_type=F32
    ).astype(BF)
    returned = all_to_all(expert_out.reshape(experts, per_peer, STEP), PLANE)
    shared_total = shared_sum(parts, tok_local)
    route_weight = 2.5 * gate_scores / jnp.sum(gate_scores, axis=1, keepdims=True)
    weight_table = jnp.sum(jnp.where(matches, route_weight[None, :, :], 0.0), axis=2).T
    spread = (
        weight_table.reshape(1, tok_local, experts, 1, capacity)
        * same_chunk.astype(F32)[:, None, None, :, None]
    ).reshape(CHUNKS * tok_local, CHUNKS * slots)
    routed_total = jnp.dot(
        spread,
        returned.reshape(CHUNKS * slots, STEP).astype(F32),
        precision=lax.Precision.HIGHEST,
    )
    routed_total = jnp.transpose(routed_total.reshape(CHUNKS, tok_local, STEP), (1, 0, 2))
    return (hidden_f + shared_total + routed_total.reshape(tok_local, D)).astype(BF)


def solution(mesh):
    grid = Mesh(mesh.devices.reshape(2, 4, 2, 8, 2), AXES)
    return jax.shard_map(
        on_device,
        mesh=grid,
        in_specs=(
            P(CTX, EXP),
            P(CTX, None),
            P(None, EXP),
            P(EXP, CTX),
            P(CTX + EXP, None),
            P(),
            P(CTX + EXP, None),
            P(CTX + EXP, None),
            P(EXP, None, None, CTX),
            P(EXP, CTX, None),
            P(None, None, CTX),
            P(CTX, None),
        ),
        out_specs=P(CTX + EXP, None),
        check_vma=False,
    )
```

```python
import functools
import math

import jax
import jax.numpy as jnp
from jax import lax
from jax.experimental import pallas as pl
from jax.experimental.pallas import tpu as pltpu
from jax.sharding import Mesh
from jax.sharding import PartitionSpec as P

D = 7168
NOPE = 128
ROPE = 64
VHD = 128
KVL = 512
TOPK = 4
BF = jnp.bfloat16
F32 = jnp.float32
AXES = ("xh", "y", "core", "z", "xl")
CTX = ("xh", "y", "core")
EXP = ("z", "xl")
PLANE = ("z", "xl", "xh")
STEP = 1792
CHUNKS = D // STEP


def swap(x, axis):
    return lax.ppermute(x, axis, [(0, 1), (1, 0)])


def shift(x, axis, by):
    n = lax.axis_size(axis)
    return lax.ppermute(x, axis, [(i, (i + by) % n) for i in range(n)])


def flip(x, axis, bits):
    return lax.ppermute(x, axis, [(i, i ^ bits) for i in range(lax.axis_size(axis))])


def near_x(x):
    return lax.ppermute(x, ("xh", "xl"), [(0, 3), (3, 0), (1, 2), (2, 1)])


def all_to_all(x, axes):
    return lax.all_to_all(x, axes, split_axis=0, concat_axis=0, tiled=True)


def gather_y(x):
    return [x, shift(x, "y", -1), shift(x, "y", 2), shift(x, "y", 1)]


def add(a, b):
    return (a.astype(F32) + b.astype(F32)).astype(BF)


def expert_kernel(in_rows, out_rows, cuts, out_cuts, n_after, *refs):
    n_in, n_out = len(in_rows) * cuts, len(out_rows) * out_cuts
    x_refs = refs[:n_in]
    gu_ref, down_ref = refs[n_in : n_in + 2]
    outs_at = n_in + 2 + n_after
    out_refs = refs[outs_at : outs_at + n_out]
    x_v, gu_v, down_v, x_sem, gu_sem, down_sem = refs[outs_at + n_out :]
    chunks, _, width = x_v.shape
    part_chunks = chunks // cuts
    steps = D // STEP
    hidden = down_ref.shape[0]
    x_copies, gu_copies = [], []
    for c in range(cuts):
        offset = 0
        for b, rows in enumerate(in_rows):
            copy = pltpu.make_async_copy(
                x_refs[b * cuts + c],
                x_v.at[pl.ds(c * part_chunks, part_chunks), pl.ds(offset, rows), :],
                x_sem.at[b * cuts + c],
            )
            copy.start()
            x_copies.append(copy)
            offset += rows
        for s in range(c * steps // cuts, (c + 1) * steps // cuts):
            span = pl.ds(s * STEP, STEP)
            copy = pltpu.make_async_copy(gu_ref.at[:, span, :], gu_v.at[:, span, :], gu_sem.at[s])
            copy.start()
            gu_copies.append(copy)
    down_copy = pltpu.make_async_copy(down_ref, down_v, down_sem)
    down_copy.start()
    acc = None
    for s in range(steps):
        if s * cuts % steps == 0:
            c = s * cuts // steps
            for copy in x_copies[c * len(in_rows) : (c + 1) * len(in_rows)]:
                copy.wait()
        gu_copies[s].wait()
        span = slice(s * STEP, (s + 1) * STEP)
        both = jnp.concatenate([gu_v[0, span, :], gu_v[1, span, :]], axis=1)
        chunk, lo = divmod(s * STEP, width)
        part = jnp.dot(x_v[chunk, :, lo : lo + STEP], both, preferred_element_type=F32)
        acc = part if acc is None else acc + part
    gate, up = acc[:, :hidden], acc[:, hidden:]
    act = (gate / (1.0 + jnp.exp(-gate)) * up).astype(BF)
    down_copy.wait()
    for s in range(steps):
        out = jnp.dot(
            act, down_v[:, s * STEP : (s + 1) * STEP], preferred_element_type=F32
        ).astype(BF)
        chunk, lo = divmod(s * STEP, width)
        part, chunk = divmod(chunk, chunks // out_cuts)
        offset = 0
        for b, rows in enumerate(out_rows):
            out_refs[b * out_cuts + part][chunk, :, lo : lo + STEP] = out[offset : offset + rows]
            offset += rows


def expert_blocks(blocks, out_rows, out_cuts, gate_up, down, after=()):
    cuts = len(blocks[0])
    in_rows = tuple(b[0].shape[1] for b in blocks)
    rows = sum(in_rows)
    hidden = down.shape[0]
    steps = D // STEP
    width = blocks[0][0].shape[2]
    chunks = D // width
    flat = pl.pallas_call(
        functools.partial(expert_kernel, in_rows, out_rows, cuts, out_cuts, len(after)),
        out_shape=[
            jax.ShapeDtypeStruct((chunks // out_cuts, r, width), BF)
            for r in out_rows
            for _ in range(out_cuts)
        ],
        in_specs=[pl.BlockSpec(memory_space=pl.ANY)] * (len(in_rows) * cuts)
        + [pl.BlockSpec(memory_space=pltpu.HBM)] * 2
        + [pl.BlockSpec(memory_space=pl.ANY)] * len(after),
        out_specs=[pl.BlockSpec(memory_space=pltpu.VMEM)] * (len(out_rows) * out_cuts),
        scratch_shapes=[
            pltpu.VMEM((chunks, rows, width), BF),
            pltpu.VMEM((2, D, hidden), BF),
            pltpu.VMEM((hidden, D), BF),
            pltpu.SemaphoreType.DMA((len(in_rows) * cuts,)),
            pltpu.SemaphoreType.DMA((steps,)),
            pltpu.SemaphoreType.DMA,
        ],
        compiler_params=pltpu.CompilerParams(vmem_limit_bytes=40 * 2**20),
        cost_estimate=pl.CostEstimate(
            flops=6 * rows * D * hidden,
            bytes_accessed=2 * (3 * D * hidden + 2 * rows * D),
            transcendentals=rows * hidden,
        ),
    )(*[part for b in blocks for part in b], gate_up, down, *after)
    return [flat[i * out_cuts : (i + 1) * out_cuts] for i in range(len(out_rows))]


def attention(queries, kv_latent, kv_up, sent):
    tok = queries.shape[0]
    heads = queries.shape[1] // (NOPE + ROPE)
    xh, y, core = (lax.axis_index(a) for a in CTX)
    pair = jnp.concatenate([kv_latent, near_x(kv_latent)], axis=0)
    chip = gather_y(pair)
    latent = jnp.concatenate(chip + [swap(p, "core") for p in chip], axis=0)
    latent, *sent = lax.optimization_barrier((latent, *sent))
    starts = []
    for c in (core, 1 - core):
        for dy in range(4):
            for x in (xh, 1 - xh):
                starts.append((x * 8 + lax.rem(y + dy, 4) * 2 + c) * tok)
    starts = jnp.stack(starts)
    key_pos = (starts[:, None] + jnp.arange(tok, dtype=jnp.int32)[None, :]).reshape(-1)
    query_heads = queries.reshape(tok, heads, NOPE + ROPE)
    seq = latent.shape[0]
    expanded = jnp.dot(latent[:, :KVL], kv_up, preferred_element_type=F32).astype(BF)
    expanded = expanded.reshape(seq, heads, NOPE + VHD)
    rope_part = jnp.broadcast_to(latent[:, None, KVL:], (seq, heads, ROPE))
    key_full = jnp.concatenate([expanded[:, :, :NOPE], rope_part], axis=2)
    scores = jnp.einsum(
        "qhc,khc->hqk", query_heads, key_full, preferred_element_type=F32
    ) / math.sqrt(NOPE + ROPE)
    query_pos = (xh * 8 + y * 2 + core) * tok + jnp.arange(tok, dtype=jnp.int32)
    allowed = (key_pos[None, :] <= query_pos[:, None])[None, :, :]
    row_max = jnp.max(jnp.where(allowed, scores, -jnp.inf), axis=2, keepdims=True)
    weights = jnp.exp(jnp.where(allowed, scores - row_max, -jnp.inf))
    weighted = jnp.einsum(
        "hqk,khv->qhv", weights.astype(BF), expanded[:, :, NOPE:], preferred_element_type=F32
    )
    total = jnp.sum(weights, axis=2).T[:, :, None]
    return (weighted / total).astype(BF).reshape(tok, heads * VHD), sent


def send_weights(out_proj):
    core = lax.axis_index("core")
    half = out_proj.shape[0] // 2
    first = core == 0
    kept = lax.dynamic_slice_in_dim(out_proj, core * half, half, 0)
    other = swap(lax.dynamic_slice_in_dim(out_proj, (1 - core) * half, half, 0), "core")
    mine = jnp.concatenate([jnp.where(first, kept, other), jnp.where(first, other, kept)], axis=1)
    a = lax.ppermute(mine, ("xh", "xl"), [(1, 0), (3, 1), (0, 2), (2, 3)])
    b = lax.ppermute(mine, ("xh", "xl"), [(2, 1), (1, 2)])
    return mine, a, b


def out_weights(mine, a, b):
    xh, core, xl = (lax.axis_index(i) for i in ("xh", "core", "xl"))
    first = core == 0
    x = 2 * xh + xl
    low = jnp.where(x == 0, mine, jnp.where(x == 1, b, a))
    high = jnp.where(x == 3, mine, jnp.where(x == 2, b, a))
    pair = jnp.concatenate([low, high], axis=0)
    theirs = swap(pair, "core")
    return jnp.concatenate([jnp.where(first, pair, theirs), jnp.where(first, theirs, pair)], axis=0)


def project(attended, weights):
    y, xl = lax.axis_index("y"), lax.axis_index("xl")
    n_y, n_z, n_xl = (lax.axis_size(a) for a in ("y", "z", "xl"))
    tok, depth = attended.shape
    half = depth // 2
    peer = swap(attended, "xl")
    left, right = jnp.where(xl == 0, attended, peer), jnp.where(xl == 0, peer, attended)
    both = jnp.concatenate(
        [left[:, :half], right[:, :half], left[:, half:], right[:, half:]], axis=1
    )
    rows = jnp.stack([both, *(flip(both, "y", j) for j in (1, 2, 3))]).reshape(n_y, n_z, tok // n_z, 2 * depth)
    rows = jnp.transpose(rows, (1, 0, 2, 3)).reshape(n_y * tok, 2 * depth)
    partial = jnp.dot(rows, weights, preferred_element_type=F32).astype(BF)
    width = partial.shape[1]
    partial = all_to_all(partial.reshape(n_z, n_y * tok // n_z, width), ("z",))
    summed = jnp.sum(partial.astype(F32), axis=0).astype(BF)
    local = summed.shape[0] // (n_y * n_xl)
    summed = summed.reshape(n_y, n_xl, local, width)
    ours = jnp.where(xl == 0, summed[:, 0], summed[:, 1])
    theirs = swap(jnp.where(xl == 0, summed[:, 1], summed[:, 0]), "xl")
    cols = jnp.stack([jnp.where(xl == 0, ours, theirs), jnp.where(xl == 0, theirs, ours)], axis=1)
    met = flip(jnp.stack([cols[1], cols[3]]), "y", 1)
    met_far = flip(jnp.stack([cols[2], met[1]]), "y", 2)
    mine = jnp.stack([cols[0], met[0], met_far[0], met_far[1]])
    mine = jnp.where(y % 2 == 0, mine, jnp.stack([mine[1], mine[0], mine[3], mine[2]]))
    mine = jnp.where(y < 2, mine, jnp.concatenate([mine[2:], mine[:2]], axis=0))
    return jnp.transpose(mine, (2, 1, 0, 3)).reshape(local, D)


def routed_ring(own, gate_up, down, early):
    left, right = own
    rows = left.shape[1]

    def other_core(block):
        return [swap(h, "core") for h in block]

    from_prev = [shift(left, "y", 1), shift(right, "y", 1)]
    from_next = [shift(left, "y", -1), shift(right, "y", -1)]
    far = [shift(from_prev[0], "y", 1), shift(from_next[1], "y", -1)]
    (keep,), (give,) = expert_blocks([own, other_core(own)], (rows, rows), 1, gate_up, down)
    from_next, from_prev, keep, early = lax.optimization_barrier((from_next, from_prev, keep, early))
    here = keep.astype(F32) + swap(give, "core").astype(F32)
    keep_n, keep_p, give_np = expert_blocks(
        [from_next, from_prev, other_core(from_next), other_core(from_prev)],
        (rows, rows, 2 * rows),
        2,
        gate_up,
        down,
        after=(keep,),
    )
    far, keep_n = lax.optimization_barrier((far, keep_n))
    got = other_core(give_np)
    to_next = [add(keep_n[c], got[c][:, :rows]) for c in range(2)]
    to_prev = [add(keep_p[c], got[c][:, rows:]) for c in range(2)]
    right_sum, left_sum = shift(to_next[1], "y", 1), shift(to_prev[0], "y", -1)
    keep, give = expert_blocks(
        [far, other_core(far)], (rows, rows), 2, gate_up, down, after=(keep_n[0],)
    )
    to_far = [add(k, g) for k, g in zip(keep, other_core(give), strict=True)]
    via_next, via_prev = shift(to_far[0], "y", 1), shift(to_far[1], "y", -1)
    next_left, prev_right = add(to_next[0], via_next), add(to_prev[1], via_prev)
    half = here.shape[0] // 2
    out_left = here[:half] + left_sum.astype(F32) + shift(next_left, "y", 1).astype(F32)
    out_right = here[half:] + right_sum.astype(F32) + shift(prev_right, "y", -1).astype(F32)
    return jnp.concatenate([out_left, out_right], axis=0).astype(BF), early


def shared_parts(normed, gate_up, down):
    rows = jnp.concatenate([normed, near_x(normed)], axis=0)
    blocks = gather_y(rows)
    theirs = swap(jnp.concatenate(blocks, axis=0), "core")
    count = theirs.shape[0]
    (keep,), (give,) = expert_blocks(
        [[b[None]] for b in [*blocks, theirs]], (count, count), 1, gate_up, down
    )
    return keep[0], give[0]


def shared_here(keep, give):
    parts = add(keep, swap(give, "core")).reshape(4, -1, D)
    local = parts.shape[1] // 2
    return add(parts[:, :local], near_x(parts[:, local:]))


def shared_sum(parts):
    return (
        parts[0].astype(F32)
        + shift(parts[1], "y", 1).astype(F32)
        + shift(parts[2], "y", 2).astype(F32)
        + shift(parts[3], "y", -1).astype(F32)
    )


def on_device(
    queries,
    kv_latent,
    kv_up,
    out_proj,
    residual,
    norm_gain,
    routes,
    gate_scores,
    expert_gate_up,
    expert_down,
    shared_gate_up,
    shared_down,
):
    attended, sent = attention(queries, kv_latent, kv_up, send_weights(out_proj))
    head_total = project(attended, out_weights(*sent))
    hidden = (residual.astype(F32) + head_total.astype(F32)).astype(BF)
    hidden_f = hidden.astype(F32)
    normed = (
        hidden_f
        * lax.rsqrt(jnp.mean(hidden_f * hidden_f, axis=1, keepdims=True) + 1e-06)
        * norm_gain
    ).astype(BF)
    tok_local = residual.shape[0]
    experts = 2 * lax.axis_size(EXP)
    capacity = min(tok_local, 2 * tok_local * TOPK // experts)
    flat_routes = routes.reshape(-1)
    order = jnp.arange(flat_routes.shape[0], dtype=jnp.int32)
    earlier = (flat_routes[:, None] == flat_routes[None, :]) & (order[None, :] < order[:, None])
    rank_within = jnp.sum(earlier.astype(jnp.int32), axis=1)
    slot_index = (flat_routes * capacity + rank_within).reshape(tok_local, TOPK)
    slots = experts * capacity
    slot_ids = jnp.arange(slots, dtype=jnp.int32)
    matches = slot_index[None, :, :] == slot_ids[:, None, None]
    placement = jnp.any(matches, axis=2).astype(BF)
    same_chunk = jnp.eye(CHUNKS, dtype=BF)
    pick = placement.reshape(experts, 1, capacity, 1, tok_local) * same_chunk[None, :, None, :, None]
    chunked = jnp.transpose(normed.reshape(tok_local, CHUNKS, STEP), (1, 0, 2)).reshape(-1, STEP)
    send_rows = jnp.dot(
        pick.reshape(CHUNKS * slots, CHUNKS * tok_local), chunked, preferred_element_type=F32
    ).astype(BF)
    per_peer = CHUNKS * capacity
    arrived = all_to_all(send_rows.reshape(experts, per_peer, STEP), PLANE)
    arrived = arrived.reshape(CHUNKS * slots, STEP)
    at = jnp.arange(CHUNKS * slots, dtype=jnp.int32)
    peer_at = at % slots // capacity * per_peer + at // slots * capacity + at % capacity
    by_chunk = (peer_at[:, None] == at[None, :]).astype(BF)
    half = CHUNKS // 2 * slots
    halves = [
        jnp.dot(rows, arrived, preferred_element_type=F32).astype(BF).reshape(-1, slots, STEP)
        for rows in (by_chunk[:half], by_chunk[half:])
    ]
    early = shared_parts(normed, shared_gate_up, shared_down)
    expert_out, early = routed_ring(halves, expert_gate_up[0], expert_down[0], early)
    parts = shared_here(*early)
    expert_out, parts = lax.optimization_barrier((expert_out, parts))
    by_peer = (at[:, None] == peer_at[None, :]).astype(BF)
    expert_out = jnp.dot(
        by_peer, expert_out.reshape(CHUNKS * slots, STEP), preferred_element_type=F32
    ).astype(BF)
    returned = all_to_all(expert_out.reshape(experts, per_peer, STEP), PLANE)
    shared_total = shared_sum(parts)
    route_weight = 2.5 * gate_scores / jnp.sum(gate_scores, axis=1, keepdims=True)
    weight_table = jnp.sum(jnp.where(matches, route_weight[None, :, :], 0.0), axis=2).T
    spread = (
        weight_table.reshape(1, tok_local, experts, 1, capacity)
        * same_chunk.astype(F32)[:, None, None, :, None]
    ).reshape(CHUNKS * tok_local, CHUNKS * slots)
    routed_total = jnp.dot(
        spread,
        returned.reshape(CHUNKS * slots, STEP).astype(F32),
        precision=lax.Precision.HIGHEST,
    )
    routed_total = jnp.transpose(routed_total.reshape(CHUNKS, tok_local, STEP), (1, 0, 2))
    return (hidden_f + shared_total + routed_total.reshape(tok_local, D)).astype(BF)


def solution(mesh):
    grid = Mesh(mesh.devices.reshape(2, 4, 2, 8, 2), AXES)
    return jax.shard_map(
        on_device,
        mesh=grid,
        in_specs=(
            P(CTX, EXP),
            P(CTX, None),
            P(None, EXP),
            P(EXP, CTX),
            P(CTX + EXP, None),
            P(),
            P(CTX + EXP, None),
            P(CTX + EXP, None),
            P(EXP, None, None, CTX),
            P(EXP, CTX, None),
            P(None, None, CTX),
            P(CTX, None),
        ),
        out_specs=P(CTX + EXP, None),
        check_vma=False,
    )
```
